32 devices in a mesh: row: 2 (over x), col: 16 (over z, y, core).
Axes of the slice: x: 2, y: 2, z: 4, core: 2. Of those that a mesh axis runs over, the one named last changes fastest.
Arguments:
- landmarks: bfloat16 [8192, 768], P(('row', 'col')), may hold values from -1 to 1
- jitter: bfloat16 [8192], P('col'), may hold values from 0.049804688 to 0.5
Outputs:
- panel: float32 [8192, 512], P('row')
- schur: float32 [8192, 8192], P('row', 'col')
The draws below stay inside these ranges and needn't reach their ends.
All inputs are finite; a program needn't handle non-finite values.
Results may differ from the reference program's by a relative error of at most 0.0003.
Values may be sent and summed in bfloat16 or wider, within the bound.
A program may use at most 128 MiB of HBM per device.

```python
import math
import jax
import jax.numpy as jnp
from jax import lax

E = 768
TILE = 512
M = 8192
N_COL = 16


def draw_landmarks(key, part):
    key = jax.random.fold_in(key, 7)
    key_centers, key_ids, key_noise = jax.random.split(key, 3)
    centers = jax.random.normal(key_centers, (64, E), jnp.float32)
    cluster_ids = jax.random.randint(key_ids, (M,), 0, 64)
    noise = jax.random.normal(key_noise, (M, E), jnp.float32)
    values = (0.8 * centers[cluster_ids] + 0.6 * noise) / jnp.sqrt(jnp.float32(E))
    return jnp.clip(values, -1.0, 1.0).astype(jnp.bfloat16)


def block_levels(stream_key, extent, shards, low, largest):
    gain, own = 1.0, jax.random.fold_in(stream_key, 6)
    for position, parts in shards:
        heights = jnp.exp(jax.random.uniform(jax.random.fold_in(own, position), (parts,), jnp.float32, low / len(shards), largest / len(shards)))
        gain = gain * jnp.repeat(heights, extent[position] // parts).reshape([-1 if axis == position else 1 for axis in range(len(extent))])
    return gain


def setup_inputs(seed: int = 0) -> dict:
    seeds = jax.random.split(jax.random.key(seed), 3)
    return {
        "landmarks": draw_landmarks(jax.random.fold_in(seeds[2], 71), 0),
        "jitter": jnp.clip(jnp.exp(math.log(0.5) - 2.306499 * jax.random.uniform(seeds[1], (M,), jnp.float32) ** block_levels(seeds[1], (M,), ((0, 16),), -0.2, 0.2)), 0.049804688, 0.5).astype(jnp.bfloat16),
    }


kernel_rate = 1.5

def gram_block(left, right, left_sq, right_sq):
    cross = lax.dot_general(left.astype(jnp.float32), right.astype(jnp.float32), (((1,), (1,)), ((), ())), preferred_element_type=jnp.float32)
    return jnp.exp(-kernel_rate * (left_sq[:, None] + right_sq[None, :] - 2.0 * cross))

def with_jitter(values, row_start, col_start, jit_values):
    row_ids = row_start + lax.broadcasted_iota(jnp.int32, values.shape, 0)
    col_ids = col_start + lax.broadcasted_iota(jnp.int32, values.shape, 1)
    return values + jnp.where(row_ids == col_ids, jit_values.astype(jnp.float32)[None, :], 0.0)

def reference(landmarks, jitter):
    squares = jnp.sum(jnp.square(landmarks.astype(jnp.float32)), axis=1)
    first = landmarks[:TILE]
    first_sq = squares[:TILE]
    first_jit = jitter[:TILE]
    top = with_jitter(gram_block(first, first, first_sq, first_sq), jnp.int32(0), jnp.int32(0), first_jit)
    factor = jnp.linalg.cholesky(top)
    columns = with_jitter(gram_block(landmarks, first, squares, first_sq), jnp.int32(0), jnp.int32(0), first_jit)
    panel = jax.scipy.linalg.solve_triangular(factor, columns.T, lower=True).T

    def one_block(start):
        rows = lax.dynamic_slice_in_dim(landmarks, start, TILE, 0)
        rows_sq = lax.dynamic_slice_in_dim(squares, start, TILE, 0)
        rows_panel = lax.dynamic_slice_in_dim(panel, start, TILE, 0)
        values = with_jitter(gram_block(rows, landmarks, rows_sq, squares), start, jnp.int32(0), jitter)
        update = lax.dot_general(rows_panel, panel, (((1,), (1,)), ((), ())), precision=lax.Precision.HIGHEST)
        return values - update
    starts = jnp.arange(N_COL, dtype=jnp.int32) * TILE
    schur = lax.map(one_block, starts).reshape(M, M)
    return (panel, schur)
```

```python
import functools

import jax
import jax.numpy as jnp
from jax import lax
from jax.experimental import pallas as pl
from jax.experimental.pallas import tpu as pltpu
from jax.sharding import PartitionSpec as P

kernel_rate = 1.5
MESH = pl.DeviceIdType.MESH
BLOCK = 128
STRIP = 8
Z_PARTS = 4
CORES = 2


def dot_t(left, right, **kwargs):
    return lax.dot_general(
        left, right, (((1,), (1,)), ((), ())), preferred_element_type=jnp.float32, **kwargs
    )


def dot_n(left, right):
    return lax.dot_general(
        left,
        right,
        (((1,), (0,)), ((), ())),
        precision=lax.Precision.HIGHEST,
        preferred_element_type=jnp.float32,
    )


def split(values):
    high = values.astype(jnp.bfloat16)
    low = (values - high.astype(jnp.float32)).astype(jnp.bfloat16)
    return high, low


def dot3_t(left, right):
    (lh, ll), (rh, rl) = left, right
    return dot_t(lh, rh) + (dot_t(lh, rl) + dot_t(ll, rh))


def squares_of(points):
    values = points.astype(jnp.float32)
    return jnp.sum(values * values, axis=1, keepdims=True)


def as_row(column):
    wide = jnp.broadcast_to(column, (column.shape[0], BLOCK))
    return wide.T[0:1, :]


def gram_of(left, right, left_sq, right_row):
    cross = dot_t(left, right)
    return jnp.exp(-kernel_rate * (left_sq + right_row - 2.0 * cross))


def on_diagonal(values, offset, jit_row):
    rows = lax.broadcasted_iota(jnp.int32, values.shape, 0)
    cols = lax.broadcasted_iota(jnp.int32, values.shape, 1)
    return values + jnp.where(rows - cols == offset, jit_row, 0.0)


def invert_block(block):
    n = BLOCK // STRIP
    sub = lax.broadcasted_iota(jnp.int32, (STRIP, BLOCK), 0)
    lane = lax.broadcasted_iota(jnp.int32, (STRIP, BLOCK), 1)
    a = [block[STRIP * i : STRIP * (i + 1), :] for i in range(n)]
    y = [jnp.where(lane == sub + STRIP * i, 1.0, 0.0).astype(jnp.float32) for i in range(n)]
    shape = (STRIP, BLOCK)
    for s in range(n):
        def column(strip, j):
            return jnp.broadcast_to(strip[:, STRIP * s + j : STRIP * s + j + 1], shape)

        r, q = a[s], y[s]
        b = [column(r, j) for j in range(STRIP)]
        rows, qrows, brows, pivots = [], [], [], []
        scale = jnp.zeros(shape, jnp.float32)
        for j in range(STRIP):
            take = lambda v: jnp.broadcast_to(v[j : j + 1, :], shape)
            inverse = 1.0 / take(b[j])
            scale = jnp.where(sub == j, inverse, scale)
            f = jnp.where(sub > j, b[j], 0.0) * inverse
            pivots.append(inverse)
            brow = {jj: take(b[jj]) for jj in range(j + 1, STRIP)}
            brows.append(brow)
            for jj in range(j + 1, STRIP):
                b[jj] = b[jj] - f * brow[jj]
            rows.append(take(r))
            qrows.append(take(q))
            r = r - f * rows[-1]
            q = q - f * qrows[-1]
        y[s] = q * lax.sqrt(scale)
        for t in range(s + 1, n):
            c = [column(a[t], j) for j in range(STRIP)]
            at, yt = a[t], y[t]
            for j in range(STRIP):
                f = c[j] * pivots[j]
                for jj in range(j + 1, STRIP):
                    c[jj] = c[jj] - f * brows[j][jj]
                at = at - f * rows[j]
                yt = yt - f * qrows[j]
            a[t], y[t] = at, yt
    return jnp.concatenate(y, axis=0)


def factor_inverse(points, jit_row, s_ref, y_ref):
    tile = points.shape[0]
    sq = squares_of(points)
    s_ref[...] = on_diagonal(gram_of(points, points, sq, as_row(sq)), 0, jit_row)
    rows = lax.broadcasted_iota(jnp.int32, (tile, tile), 0)
    cols = lax.broadcasted_iota(jnp.int32, (tile, tile), 1)
    y_ref[...] = jnp.where(rows == cols, 1.0, 0.0).astype(jnp.float32)

    def step(block, carry):
        here = pl.ds(pl.multiple_of(block * BLOCK, BLOCK), BLOCK)
        v = invert_block(s_ref[here, here])
        u = dot_n(v, s_ref[here, :])
        x = dot_n(v, y_ref[here, :])
        below = dot_t(s_ref[:, here], v, precision=lax.Precision.HIGHEST)
        ids = lax.broadcasted_iota(jnp.int32, below.shape, 0)
        below = jnp.where(ids >= (block + 1) * BLOCK, below, 0.0)
        s_ref[...] -= dot_n(below, u)
        y_ref[...] -= dot_n(below, x)
        y_ref[here, :] = x
        return carry

    lax.fori_loop(0, tile // BLOCK, step, 0)


def factor_kernel(points_ref, jit_ref, high_ref, low_ref, s_ref, y_ref):
    factor_inverse(points_ref[...], jit_ref[0:1, :], s_ref, y_ref)
    high_ref[...], low_ref[...] = split(y_ref[...])


def factor_call(points, jit):
    tile = points.shape[0]
    out = jax.ShapeDtypeStruct((tile, tile), jnp.bfloat16)
    return pl.pallas_call(
        factor_kernel,
        out_shape=(out, out),
        scratch_shapes=[pltpu.VMEM((tile, tile), jnp.float32)] * 2,
        compiler_params=pltpu.CompilerParams(vmem_limit_bytes=32 << 20),
        name="factor",
    )(points, jit)


def schur_kernel(per_row, rows_ref, cols_ref, first_ref, xh_ref, xl_ref, jit_ref, first_jit_ref,
                 panel_ref, schur_ref, col_row_ref, first_row_ref, ph_ref, pl_ref):
    step = pl.program_id(0)
    row_index = lax.axis_index("row")
    col_index = lax.axis_index("col")
    bm = rows_ref.shape[0]
    tile = cols_ref.shape[0]
    row_start = (row_index * pl.num_programs(0) + step) * bm
    col_start = col_index * tile
    inverse = (xh_ref[...], xl_ref[...])

    @pl.when(step == 0)
    def _():
        col_sq = squares_of(cols_ref[...])
        col_row_ref[...] = as_row(col_sq)
        first_row_ref[...] = as_row(squares_of(first_ref[...]))
        part = gram_of(cols_ref[...], first_ref[...], col_sq, first_row_ref[...])
        part = on_diagonal(part, -col_start, first_jit_ref[0:1, :])
        ph_ref[...], pl_ref[...] = split(dot3_t(split(part), inverse))

    points = rows_ref[...]
    sq = squares_of(points)
    part = gram_of(points, first_ref[...], sq, first_row_ref[...])
    part = on_diagonal(part, -row_start, first_jit_ref[0:1, :])
    panel = dot3_t(split(part), inverse)
    panel_ref[...] = panel
    block = gram_of(points, cols_ref[...], sq, col_row_ref[...])
    block = on_diagonal(block, col_start - row_start, jit_ref[0:1, :])
    schur_ref[...] = block - dot3_t(split(panel), (ph_ref[...], pl_ref[...]))


def schur_call(per_row, row_pts, col_pts, first_pts, xh, xl, jit, first_jit):
    rowb, width = row_pts.shape
    tile = col_pts.shape[0]
    bm = min(512, rowb)
    whole = lambda shape: pl.BlockSpec(shape, lambda i: (0, 0))
    out = jax.ShapeDtypeStruct((rowb, tile), jnp.float32)
    return pl.pallas_call(
        functools.partial(schur_kernel, per_row),
        grid=(rowb // bm,),
        in_specs=[
            pl.BlockSpec((bm, width), lambda i: (i, 0)),
            whole((tile, width)),
            whole((tile, width)),
            whole((tile, tile)),
            whole((tile, tile)),
            whole((8, tile)),
            whole((8, tile)),
        ],
        out_specs=[pl.BlockSpec((bm, tile), lambda i: (i, 0))] * 2,
        out_shape=(out, out),
        scratch_shapes=[
            pltpu.VMEM((1, tile), jnp.float32),
            pltpu.VMEM((1, tile), jnp.float32),
            pltpu.VMEM((tile, tile), jnp.bfloat16),
            pltpu.VMEM((tile, tile), jnp.bfloat16),
        ],
        compiler_params=pltpu.CompilerParams(vmem_limit_bytes=48 << 20),
        name="schur",
    )(row_pts, col_pts, first_pts, xh, xl, jit, first_jit)


def gather_kernel(rows, cols, own_ref, jit_ref, out_ref, col_ref, first_ref, first_jit_ref,
                  send_z, send_y, send_k, recv, send_x, recv_x, send_f, recv_f, send_fk,
                  recv_fk, send_j, recv_j, local):
    me_row = lax.axis_index("row")
    me = lax.axis_index("col")
    size = own_ref.shape[0]
    tile = col_ref.shape[0]
    spc = tile // size
    per_row = cols // rows
    y_parts = cols // (Z_PARTS * CORES)
    core = lax.rem(me, CORES)
    my_y = lax.rem(me // CORES, y_parts)
    my_z = me // (CORES * y_parts)
    sibling = me + 1 - 2 * core

    def index(z, y, k):
        return (z * y_parts + y) * CORES + k

    def z_peer(d):
        return lax.rem(my_z + d, Z_PARTS)

    def y_peer(d):
        return lax.rem(my_y + d, y_parts)

    def row_peer(d):
        return lax.rem(me_row + d, rows)

    shard = me_row * cols + me
    tile_of = shard // spc
    place = lax.rem(shard, spc)
    home = me // per_row

    def part(ref, i, count=1):
        return ref.at[pl.ds(pl.multiple_of(i * size, size), count * size)]

    def tell(row, col):
        pl.semaphore_signal(
            barrier, inc=1, device_id=(row, col), device_id_type=MESH
        )

    barrier = pltpu.get_barrier_semaphore()
    tell(me_row, sibling)
    for d in range(1, Z_PARTS):
        tell(me_row, index(z_peer(d), my_y, core))
    for d in range(1, y_parts):
        tell(me_row, index(my_z, y_peer(d), core))
    count = 1 + (Z_PARTS - 1) + (y_parts - 1)
    for d in range(1, rows):
        tell(row_peer(d), me)
    count += rows - 1
    for i in range(spc):
        source = me * spc + i
        source_row = source // cols

        @pl.when(source_row != me_row)
        def _():
            tell(source_row, lax.rem(source, cols))
    count += rows - 1

    @pl.when(me != 0)
    def _():
        tell(me_row, 0)

    @pl.when(me != 0)
    def _():
        pl.semaphore_wait(barrier, count)

    @pl.when(me == 0)
    def _():
        pl.semaphore_wait(barrier, count + cols - 1)

    def remote(src, dst, send, recv_sem, row, col):
        return pltpu.make_async_remote_copy(
            src_ref=src, dst_ref=dst, send_sem=send, recv_sem=recv_sem,
            device_id=(row, col), device_id_type=MESH,
        )

    def landed(dst, recv_sem):
        remote(dst, dst, send_j.at[0], recv_sem, me_row, sibling).wait_recv()

    own = part(out_ref, me)
    sends = []

    def go(*args):
        copy = remote(*args)
        copy.start()
        sends.append(copy)

    for d in range(1, Z_PARTS):
        go(own_ref, own, send_z.at[d], recv.at[me], me_row, index(z_peer(d), my_y, core))
    for d in range(1, y_parts):
        go(own_ref, own, send_y.at[0, d], recv.at[me], me_row, index(my_z, y_peer(d), core))
    go(own_ref, own, send_k.at[0, 0], recv.at[me], me_row, sibling)
    for d in range(1, rows):
        go(own_ref, part(col_ref, place), send_x.at[d], recv_x.at[place], row_peer(d), tile_of)

    @pl.when(me == 0)
    def _():
        for c in range(1, cols):
            remote(jit_ref, first_jit_ref, send_j.at[c], recv_j, me_row, c).start()
        copy = pltpu.make_async_copy(jit_ref, first_jit_ref, local.at[1])
        copy.start()
        copy.wait()

    mine = pltpu.make_async_copy(own_ref, own, local.at[0])
    mine.start()

    for i, dz in enumerate((1, Z_PARTS - 1, 2)):
        source = index(z_peer(dz), my_y, core)
        landed(part(out_ref, source), recv.at[source])
        for d in range(1, y_parts):
            go(part(out_ref, source), part(out_ref, source), send_y.at[dz, d], recv.at[source],
               me_row, index(my_z, y_peer(d), core))
        go(part(out_ref, source), part(out_ref, source), send_k.at[dz, 0], recv.at[source],
           me_row, sibling)
    mine.wait()
    for dz in (0, 1, Z_PARTS - 1, 2):
        for d in range(1, y_parts):
            source = index(z_peer(dz), y_peer(d), core)
            landed(part(out_ref, source), recv.at[source])
            go(part(out_ref, source), part(out_ref, source), send_k.at[dz, d], recv.at[source],
               me_row, sibling)
    for dz in range(Z_PARTS):
        for d in range(y_parts):
            source = index(z_peer(dz), y_peer(d), 1 - core)
            landed(part(out_ref, source), recv.at[source])

    half = tile // CORES

    def piece(ref, k):
        return ref.at[pl.ds(pl.multiple_of(k * half, half), half)]

    @pl.when(me_row == 0)
    def _():
        copy = pltpu.make_async_copy(out_ref.at[pl.ds(0, tile)], first_ref, local.at[2])
        copy.start()
        for d in range(1, rows):
            remote(piece(out_ref, core), piece(first_ref, core), send_f.at[d], recv_f,
                   d, me).start()
        copy.wait()
        for d in range(1, rows):
            remote(piece(out_ref, core), piece(first_ref, core), send_f.at[d], recv_f,
                   d, me).wait_send()

    @pl.when(me_row != 0)
    def _():
        landed(piece(first_ref, core), recv_f)
        copy = remote(piece(first_ref, core), piece(first_ref, core), send_fk, recv_fk,
                      me_row, sibling)
        copy.start()
        copy.wait_send()
        landed(piece(first_ref, 1 - core), recv_fk)

    @pl.when(home == me_row)
    def _():
        start = pl.multiple_of(lax.rem(me, per_row) * tile, tile)
        copy = pltpu.make_async_copy(out_ref.at[pl.ds(start, tile)], col_ref, local.at[3])
        copy.start()
        copy.wait()

    @pl.when(home != me_row)
    def _():
        for i in range(spc):
            landed(part(col_ref, i), recv_x.at[i])

    @pl.when(me == 0)
    def _():
        for c in range(1, cols):
            remote(jit_ref, first_jit_ref, send_j.at[c], recv_j, me_row, c).wait_send()

    @pl.when(me != 0)
    def _():
        landed(first_jit_ref, recv_j)

    for copy in sends:
        copy.wait_send()


def gather_call(rows, cols, landmarks, jit):
    size, width = landmarks.shape
    tile = jit.shape[1]
    y_parts = cols // (Z_PARTS * CORES)
    dma = pltpu.SemaphoreType.DMA
    return pl.pallas_call(
        functools.partial(gather_kernel, rows, cols),
        in_specs=[pl.BlockSpec(memory_space=pl.ANY)] * 2,
        out_specs=[pl.BlockSpec(memory_space=pl.ANY)] * 4,
        out_shape=(
            jax.ShapeDtypeStruct((cols * size, width), landmarks.dtype),
            jax.ShapeDtypeStruct((tile, width), landmarks.dtype),
            jax.ShapeDtypeStruct((tile, width), landmarks.dtype),
            jax.ShapeDtypeStruct(jit.shape, jit.dtype),
        ),
        scratch_shapes=[
            dma((Z_PARTS,)),
            dma((Z_PARTS, y_parts)),
            dma((Z_PARTS, y_parts)),
            dma((cols,)),
            dma((rows,)),
            dma((tile // size,)),
            dma((rows,)),
            dma,
            dma,
            dma,
            dma((cols,)),
            dma,
            dma((4,)),
        ],
        compiler_params=pltpu.CompilerParams(collective_id=0, has_side_effects=True),
        name="gather",
    )(landmarks, jit)


def local(landmarks, jitter):
    rows = lax.axis_size("row")
    cols = lax.axis_size("col")
    tile = jitter.shape[0]
    jit = jnp.broadcast_to(jitter.astype(jnp.float32)[None, :], (8, tile))
    row_pts, col_pts, first_pts, first_jit = gather_call(rows, cols, landmarks, jit)
    xh, xl = factor_call(first_pts, first_jit)
    return tuple(schur_call(cols // rows, row_pts, col_pts, first_pts, xh, xl, jit, first_jit))


def solution(mesh):
    in_specs = (P(("row", "col"), None), P("col"))
    out_specs = (P("row", None), P("row", "col"))
    return jax.shard_map(local, mesh=mesh, in_specs=in_specs, out_specs=out_specs, check_vma=False)
```

```python
import functools

import jax
import jax.numpy as jnp
from jax import lax
from jax.experimental import pallas as pl
from jax.experimental.pallas import tpu as pltpu
from jax.sharding import PartitionSpec as P

kernel_rate = 1.5
MESH = pl.DeviceIdType.MESH
BLOCK = 128
STRIP = 8
Z_PARTS = 4
CORES = 2
CHUNKS = 2


def dot_t(left, right, **kwargs):
    return lax.dot_general(
        left, right, (((1,), (1,)), ((), ())), preferred_element_type=jnp.float32, **kwargs
    )


def dot_n(left, right):
    return lax.dot_general(
        left,
        right,
        (((1,), (0,)), ((), ())),
        precision=lax.Precision.HIGHEST,
        preferred_element_type=jnp.float32,
    )


def split(values):
    high = values.astype(jnp.bfloat16)
    low = (values - high.astype(jnp.float32)).astype(jnp.bfloat16)
    return high, low


def dot3_t(left, right):
    (lh, ll), (rh, rl) = left, right
    return dot_t(lh, rh) + (dot_t(lh, rl) + dot_t(ll, rh))


def squares_of(points):
    values = points.astype(jnp.float32)
    return jnp.sum(values * values, axis=1, keepdims=True)


def as_row(column):
    wide = jnp.broadcast_to(column, (column.shape[0], BLOCK))
    return wide.T[0:1, :]


def gram_of(left, right, left_sq, right_row):
    cross = dot_t(left, right)
    return jnp.exp(-kernel_rate * (left_sq + right_row - 2.0 * cross))


def on_diagonal(values, offset, jit_row):
    rows = lax.broadcasted_iota(jnp.int32, values.shape, 0)
    cols = lax.broadcasted_iota(jnp.int32, values.shape, 1)
    return values + jnp.where(rows - cols == offset, jit_row, 0.0)


def invert_block(block):
    n = BLOCK // STRIP
    sub = lax.broadcasted_iota(jnp.int32, (STRIP, BLOCK), 0)
    lane = lax.broadcasted_iota(jnp.int32, (STRIP, BLOCK), 1)
    a = [block[STRIP * i : STRIP * (i + 1), :] for i in range(n)]
    y = [jnp.where(lane == sub + STRIP * i, 1.0, 0.0).astype(jnp.float32) for i in range(n)]
    shape = (STRIP, BLOCK)
    for s in range(n):
        def column(strip, j):
            return jnp.broadcast_to(strip[:, STRIP * s + j : STRIP * s + j + 1], shape)

        r, q = a[s], y[s]
        b = [column(r, j) for j in range(STRIP)]
        rows, qrows, brows, pivots = [], [], [], []
        scale = jnp.zeros(shape, jnp.float32)
        for j in range(STRIP):
            take = lambda v: jnp.broadcast_to(v[j : j + 1, :], shape)
            inverse = 1.0 / take(b[j])
            scale = jnp.where(sub == j, inverse, scale)
            f = jnp.where(sub > j, b[j], 0.0) * inverse
            pivots.append(inverse)
            brow = {jj: take(b[jj]) for jj in range(j + 1, STRIP)}
            brows.append(brow)
            for jj in range(j + 1, STRIP):
                b[jj] = b[jj] - f * brow[jj]
            rows.append(take(r))
            qrows.append(take(q))
            r = r - f * rows[-1]
            q = q - f * qrows[-1]
        y[s] = q * lax.sqrt(scale)
        for t in range(s + 1, n):
            c = [column(a[t], j) for j in range(STRIP)]
            at, yt = a[t], y[t]
            for j in range(STRIP):
                f = c[j] * pivots[j]
                for jj in range(j + 1, STRIP):
                    c[jj] = c[jj] - f * brows[j][jj]
                at = at - f * rows[j]
                yt = yt - f * qrows[j]
            a[t], y[t] = at, yt
    return jnp.concatenate(y, axis=0)


def factor_inverse(points, jit_row, s_ref, y_ref, between):
    tile = points.shape[0]
    sq = squares_of(points)
    s_ref[...] = on_diagonal(gram_of(points, points, sq, as_row(sq)), 0, jit_row)
    rows = lax.broadcasted_iota(jnp.int32, (tile, tile), 0)
    cols = lax.broadcasted_iota(jnp.int32, (tile, tile), 1)
    y_ref[...] = jnp.where(rows == cols, 1.0, 0.0).astype(jnp.float32)

    def step(block, carry):
        here = pl.ds(pl.multiple_of(block * BLOCK, BLOCK), BLOCK)
        v = invert_block(s_ref[here, here])
        u = dot_n(v, s_ref[here, :])
        x = dot_n(v, y_ref[here, :])
        below = dot_t(s_ref[:, here], v, precision=lax.Precision.HIGHEST)
        ids = lax.broadcasted_iota(jnp.int32, below.shape, 0)
        below = jnp.where(ids >= (block + 1) * BLOCK, below, 0.0)
        s_ref[...] -= dot_n(below, u)
        y_ref[...] -= dot_n(below, x)
        y_ref[here, :] = x
        between(block)
        return carry

    lax.fori_loop(0, tile // BLOCK, step, 0)


def schur_kernel(per_row, rows_ref, cols_ref, first_ref, xh_ref, xl_ref, jit_ref, first_jit_ref,
                 panel_ref, schur_ref, col_row_ref, first_row_ref, ph_ref, pl_ref):
    step = pl.program_id(0)
    row_index = lax.axis_index("row")
    col_index = lax.axis_index("col")
    bm = rows_ref.shape[0]
    tile = cols_ref.shape[0]
    row_start = (row_index * pl.num_programs(0) + step) * bm
    col_start = col_index * tile
    inverse = (xh_ref[...], xl_ref[...])

    @pl.when(step == 0)
    def _():
        col_sq = squares_of(cols_ref[...])
        col_row_ref[...] = as_row(col_sq)
        first_row_ref[...] = as_row(squares_of(first_ref[...]))
        part = gram_of(cols_ref[...], first_ref[...], col_sq, first_row_ref[...])
        part = on_diagonal(part, -col_start, first_jit_ref[0:1, :])
        ph_ref[...], pl_ref[...] = split(dot3_t(split(part), inverse))

    points = rows_ref[...]
    sq = squares_of(points)
    part = gram_of(points, first_ref[...], sq, first_row_ref[...])
    part = on_diagonal(part, -row_start, first_jit_ref[0:1, :])
    panel = dot3_t(split(part), inverse)
    panel_ref[...] = panel
    block = gram_of(points, cols_ref[...], sq, col_row_ref[...])
    block = on_diagonal(block, col_start - row_start, jit_ref[0:1, :])
    schur_ref[...] = block - dot3_t(split(panel), (ph_ref[...], pl_ref[...]))


def schur_call(per_row, row_pts, col_pts, first_pts, xh, xl, jit, first_jit):
    rowb, width = row_pts.shape
    tile = col_pts.shape[0]
    bm = min(512, rowb)
    whole = lambda shape: pl.BlockSpec(shape, lambda i: (0, 0))
    out = jax.ShapeDtypeStruct((rowb, tile), jnp.float32)
    return pl.pallas_call(
        functools.partial(schur_kernel, per_row),
        grid=(rowb // bm,),
        in_specs=[
            pl.BlockSpec((bm, width), lambda i: (i, 0)),
            whole((tile, width)),
            whole((tile, width)),
            whole((tile, tile)),
            whole((tile, tile)),
            whole((8, tile)),
            whole((8, tile)),
        ],
        out_specs=[pl.BlockSpec((bm, tile), lambda i: (i, 0))] * 2,
        out_shape=(out, out),
        scratch_shapes=[
            pltpu.VMEM((1, tile), jnp.float32),
            pltpu.VMEM((1, tile), jnp.float32),
            pltpu.VMEM((tile, tile), jnp.bfloat16),
            pltpu.VMEM((tile, tile), jnp.bfloat16),
        ],
        compiler_params=pltpu.CompilerParams(vmem_limit_bytes=48 << 20),
        name="schur",
    )(row_pts, col_pts, first_pts, xh, xl, jit, first_jit)


def gather_kernel(rows, cols, own_ref, jit_ref, out_ref, col_ref, first_ref, first_jit_ref,
                  high_ref, low_ref, s_ref, y_ref, send_up, send_down, send_y, send_k, recv,
                  send_x, recv_x, send_f, recv_f, send_fk, send_j, recv_j, local):
    me_row = lax.axis_index("row")
    me = lax.axis_index("col")
    size = own_ref.shape[0]
    tile = col_ref.shape[0]
    spc = tile // size
    per_row = cols // rows
    y_parts = cols // (Z_PARTS * CORES)
    core = lax.rem(me, CORES)
    my_y = lax.rem(me // CORES, y_parts)
    my_z = me // (CORES * y_parts)
    sibling = me + 1 - 2 * core
    chunk = size // CHUNKS

    def index(z, y, k):
        return (z * y_parts + y) * CORES + k

    def y_peer(d):
        return lax.rem(my_y + d, y_parts)

    def row_peer(d):
        return lax.rem(me_row + d, rows)

    shard = me_row * cols + me
    tile_of = shard // spc
    place = lax.rem(shard, spc)
    home = me // per_row

    def part(ref, i, h):
        return ref.at[pl.ds(pl.multiple_of(i * size + h * chunk, chunk), chunk)]

    def whole(ref, i):
        return ref.at[pl.ds(pl.multiple_of(i * size, size), size)]

    def tell(row, col):
        pl.semaphore_signal(barrier, inc=1, device_id=(row, col), device_id_type=MESH)

    barrier = pltpu.get_barrier_semaphore()
    tell(me_row, sibling)

    @pl.when(my_z > 0)
    def _():
        tell(me_row, index(my_z - 1, my_y, core))

    @pl.when(my_z < Z_PARTS - 1)
    def _():
        tell(me_row, index(my_z + 1, my_y, core))

    for d in range(1, y_parts):
        tell(me_row, index(my_z, y_peer(d), core))
    for d in range(1, rows):
        tell(row_peer(d), me)
    for i in range(spc):
        source = me * spc + i
        source_row = source // cols

        @pl.when(source_row != me_row)
        def _():
            tell(source_row, lax.rem(source, cols))

    @pl.when(me != 0)
    def _():
        tell(me_row, 0)

    inner = 1 + 2 + (y_parts - 1) + 2 * (rows - 1)
    ends = (Z_PARTS - 1) * CORES * y_parts

    @pl.when(me == 0)
    def _():
        pl.semaphore_wait(barrier, inner - 1 + cols - 1)

    @pl.when((me != 0) & ((my_z == 0) | (me >= ends)))
    def _():
        pl.semaphore_wait(barrier, inner - 1)

    @pl.when((my_z > 0) & (me < ends))
    def _():
        pl.semaphore_wait(barrier, inner)

    def remote(src, dst, send, recv_sem, row, col):
        return pltpu.make_async_remote_copy(
            src_ref=src, dst_ref=dst, send_sem=send, recv_sem=recv_sem,
            device_id=(row, col), device_id_type=MESH,
        )

    def landed(dst, recv_sem):
        remote(dst, dst, send_j.at[0], recv_sem, me_row, sibling).wait_recv()

    def up(src, z, i, h):
        return remote(src, part(out_ref, i, h), send_up.at[z, h], recv.at[i, h],
                      me_row, index(my_z + 1, my_y, core))

    def down(src, z, i, h):
        return remote(src, part(out_ref, i, h), send_down.at[z, h], recv.at[i, h],
                      me_row, index(my_z - 1, my_y, core))

    def aside(src, z, d, i, h):
        return remote(src, part(out_ref, i, h), send_y.at[z, d, h], recv.at[i, h],
                      me_row, index(my_z, y_peer(d), core))

    def across(src, z, y, h):
        i = index(z, y, core)
        return remote(src, part(out_ref, i, h), send_k.at[z, y, h], recv.at[i, h],
                      me_row, sibling)

    def walk(act, wait):
        def spread(source, z, h, upward, downward):
            i = index(z, my_y, core)
            src = part(own_ref, 0, h) if source is own_ref else part(out_ref, i, h)
            if wait:
                landed(part(out_ref, i, h), recv.at[i, h])
            if upward:
                @pl.when(my_z < Z_PARTS - 1)
                def _():
                    act(up(src, z, i, h))
            if downward:
                @pl.when(my_z > 0)
                def _():
                    act(down(src, z, i, h))
            for d in range(1, y_parts):
                act(aside(src, z, d, i, h))
            act(across(src, z, my_y, h))

        for d in range(1, Z_PARTS):
            for h in range(CHUNKS):
                @pl.when(my_z >= d)
                def _():
                    spread(out_ref, my_z - d, h, True, False)

                @pl.when(my_z + d < Z_PARTS)
                def _():
                    spread(out_ref, my_z + d, h, False, True)

    def own_copies(act):
        for h in range(CHUNKS):
            src = part(own_ref, 0, h)

            @pl.when(my_z < Z_PARTS - 1)
            def _():
                act(up(src, my_z, me, h))

            @pl.when(my_z > 0)
            def _():
                act(down(src, my_z, me, h))

            for d in range(1, y_parts):
                act(aside(src, my_z, d, me, h))
            act(across(src, my_z, my_y, h))

    def to_columns(d):
        return remote(own_ref, whole(col_ref, place), send_x.at[d], recv_x.at[place],
                      row_peer(d), tile_of)

    def jit_copy(c):
        return remote(jit_ref, first_jit_ref, send_j.at[c], recv_j, me_row, c)

    def begin(copy):
        copy.start()

    def finish(copy):
        copy.wait_send()

    own_copies(begin)
    mine = pltpu.make_async_copy(own_ref, whole(out_ref, me), local.at[0])
    mine.start()

    @pl.when(me == 0)
    def _():
        for c in range(1, cols):
            jit_copy(c).start()
        copy = pltpu.make_async_copy(jit_ref, first_jit_ref, local.at[1])
        copy.start()
        copy.wait()

    walk(begin, True)
    mine.wait()

    def first_copy(d, s, h):
        return remote(part(out_ref, s, h), part(first_ref, s, h), send_f.at[d, s, h],
                      recv_f.at[s, h], d, me)

    def first_across(s, h):
        return remote(part(first_ref, s, h), part(first_ref, s, h), send_fk.at[s, h],
                      recv_f.at[s, h], me_row, sibling)

    ahead = spc // CORES
    for y in range(ahead):
        s = index(0, y, core)
        for h in range(CHUNKS):
            @pl.when(my_y != y)
            def _():
                landed(part(out_ref, s, h), recv.at[s, h])
                across(part(out_ref, s, h), 0, y, h).start()

            @pl.when(me_row == 0)
            def _():
                for d in range(1, rows):
                    first_copy(d, s, h).start()
    for y in range(ahead):
        s = index(0, y, core)
        for h in range(CHUNKS):
            @pl.when(me_row != 0)
            def _():
                landed(part(first_ref, s, h), recv_f.at[s, h])
                first_across(s, h).start()

    for d in range(1, rows):
        to_columns(d).start()

    for y in range(ahead):
        s = index(0, y, 1 - core)
        for h in range(CHUNKS):
            landed(part(out_ref, s, h), recv.at[s, h])

            @pl.when(me_row != 0)
            def _():
                landed(part(first_ref, s, h), recv_f.at[s, h])

    @pl.when(me_row == 0)
    def _():
        copy = pltpu.make_async_copy(out_ref.at[pl.ds(0, tile)], first_ref, local.at[2])
        copy.start()
        copy.wait()

    @pl.when(me != 0)
    def _():
        landed(first_jit_ref, recv_j)

    def pass_on(z):
        for d in range(1, y_parts):
            y = y_peer(d)
            i = index(z, y, core)

            @pl.when(i >= spc)
            def _():
                for h in range(CHUNKS):
                    landed(part(out_ref, i, h), recv.at[i, h])
                    across(part(out_ref, i, h), z, y, h).start()

    blocks = tile // BLOCK

    def between(block):
        @pl.when(block < Z_PARTS)
        def _():
            pass_on(block)

    factor_inverse(first_ref[...], first_jit_ref[0:1, :], s_ref, y_ref, between)
    high_ref[...], low_ref[...] = split(y_ref[...])
    for z in range(blocks, Z_PARTS):
        pass_on(z)

    for z in range(Z_PARTS):
        for y in range(y_parts):
            if index(z, y, 0) >= spc:
                i = index(z, y, 1 - core)
                for h in range(CHUNKS):
                    landed(part(out_ref, i, h), recv.at[i, h])

    @pl.when(home == me_row)
    def _():
        start = pl.multiple_of(lax.rem(me, per_row) * tile, tile)
        copy = pltpu.make_async_copy(out_ref.at[pl.ds(start, tile)], col_ref, local.at[3])
        copy.start()
        copy.wait()

    @pl.when(home != me_row)
    def _():
        for i in range(spc):
            landed(whole(col_ref, i), recv_x.at[i])

    own_copies(finish)
    walk(finish, False)
    for z in range(Z_PARTS):
        for d in range(1, y_parts):
            for h in range(CHUNKS):
                y = y_peer(d)
                finish(across(part(out_ref, index(z, y, core), h), z, y, h))
    for d in range(1, rows):
        finish(to_columns(d))
    for y in range(ahead):
        s = index(0, y, core)
        for h in range(CHUNKS):
            @pl.when(me_row == 0)
            def _():
                for d in range(1, rows):
                    finish(first_copy(d, s, h))

            @pl.when(me_row != 0)
            def _():
                finish(first_across(s, h))

    @pl.when(me == 0)
    def _():
        for c in range(1, cols):
            finish(jit_copy(c))


def gather_call(rows, cols, landmarks, jit):
    size, width = landmarks.shape
    tile = jit.shape[1]
    spc = tile // size
    y_parts = cols // (Z_PARTS * CORES)
    dma = pltpu.SemaphoreType.DMA
    vmem = pl.BlockSpec(memory_space=pltpu.VMEM)
    hbm = pl.BlockSpec(memory_space=pl.ANY)
    return pl.pallas_call(
        functools.partial(gather_kernel, rows, cols),
        in_specs=[hbm, vmem],
        out_specs=[hbm, hbm, vmem, vmem, vmem, vmem],
        out_shape=(
            jax.ShapeDtypeStruct((cols * size, width), landmarks.dtype),
            jax.ShapeDtypeStruct((tile, width), landmarks.dtype),
            jax.ShapeDtypeStruct((tile, width), landmarks.dtype),
            jax.ShapeDtypeStruct(jit.shape, jit.dtype),
            jax.ShapeDtypeStruct((tile, tile), jnp.bfloat16),
            jax.ShapeDtypeStruct((tile, tile), jnp.bfloat16),
        ),
        scratch_shapes=[
            pltpu.VMEM((tile, tile), jnp.float32),
            pltpu.VMEM((tile, tile), jnp.float32),
            dma((Z_PARTS, CHUNKS)),
            dma((Z_PARTS, CHUNKS)),
            dma((Z_PARTS, y_parts, CHUNKS)),
            dma((Z_PARTS, y_parts, CHUNKS)),
            dma((cols, CHUNKS)),
            dma((rows,)),
            dma((spc,)),
            dma((rows, spc, CHUNKS)),
            dma((spc, CHUNKS)),
            dma((spc, CHUNKS)),
            dma((cols,)),
            dma,
            dma((4,)),
        ],
        compiler_params=pltpu.CompilerParams(
            collective_id=0, has_side_effects=True, vmem_limit_bytes=32 << 20
        ),
        name="gather",
    )(landmarks, jit)


def local(landmarks, jitter):
    rows = lax.axis_size("row")
    cols = lax.axis_size("col")
    tile = jitter.shape[0]
    jit = jnp.broadcast_to(jitter.astype(jnp.float32)[None, :], (8, tile))
    row_pts, col_pts, first_pts, first_jit, xh, xl = gather_call(rows, cols, landmarks, jit)
    return tuple(schur_call(cols // rows, row_pts, col_pts, first_pts, xh, xl, jit, first_jit))


def solution(mesh):
    in_specs = (P(("row", "col"), None), P("col"))
    out_specs = (P("row", None), P("row", "col"))
    return jax.shard_map(local, mesh=mesh, in_specs=in_specs, out_specs=out_specs, check_vma=False)
```

```python
import functools

import jax
import jax.numpy as jnp
from jax import lax
from jax.experimental import pallas as pl
from jax.experimental.pallas import tpu as pltpu
from jax.sharding import PartitionSpec as P

kernel_rate = 1.5
MESH = pl.DeviceIdType.MESH
BLOCK = 128
STRIP = 8
Z_PARTS = 4
CORES = 2
CHUNKS = 4
ORDER = ((1, 2, 3), (0, 2, 3), (3, 0, 1), (2, 0, 1))


def dot_t(left, right, **kwargs):
    return lax.dot_general(
        left, right, (((1,), (1,)), ((), ())), preferred_element_type=jnp.float32, **kwargs
    )


def dot_n(left, right):
    return lax.dot_general(
        left,
        right,
        (((1,), (0,)), ((), ())),
        precision=lax.Precision.HIGHEST,
        preferred_element_type=jnp.float32,
    )


def split(values):
    high = values.astype(jnp.bfloat16)
    low = (values - high.astype(jnp.float32)).astype(jnp.bfloat16)
    return high, low


def dot3_t(left, right):
    (lh, ll), (rh, rl) = left, right
    return dot_t(lh, rh) + (dot_t(lh, rl) + dot_t(ll, rh))


def squares_of(points):
    values = points.astype(jnp.float32)
    return jnp.sum(values * values, axis=1, keepdims=True)


def as_row(column):
    wide = jnp.broadcast_to(column, (column.shape[0], BLOCK))
    return wide.T[0:1, :]


def gram_of(left, right, left_sq, right_row):
    cross = dot_t(left, right)
    return jnp.exp(-kernel_rate * (left_sq + right_row - 2.0 * cross))


def on_diagonal(values, offset, jit_row):
    rows = lax.broadcasted_iota(jnp.int32, values.shape, 0)
    cols = lax.broadcasted_iota(jnp.int32, values.shape, 1)
    return values + jnp.where(rows - cols == offset, jit_row, 0.0)


def invert_block(block):
    n = BLOCK // STRIP
    sub = lax.broadcasted_iota(jnp.int32, (STRIP, BLOCK), 0)
    lane = lax.broadcasted_iota(jnp.int32, (STRIP, BLOCK), 1)
    a = [block[STRIP * i : STRIP * (i + 1), :] for i in range(n)]
    y = [jnp.where(lane == sub + STRIP * i, 1.0, 0.0).astype(jnp.float32) for i in range(n)]
    shape = (STRIP, BLOCK)
    for s in range(n):
        def column(strip, j):
            return jnp.broadcast_to(strip[:, STRIP * s + j : STRIP * s + j + 1], shape)

        r, q = a[s], y[s]
        b = [column(r, j) for j in range(STRIP)]
        rows, qrows, brows, pivots = [], [], [], []
        scale = jnp.zeros(shape, jnp.float32)
        for j in range(STRIP):
            take = lambda v: jnp.broadcast_to(v[j : j + 1, :], shape)
            inverse = 1.0 / take(b[j])
            scale = jnp.where(sub == j, inverse, scale)
            f = jnp.where(sub > j, b[j], 0.0) * inverse
            pivots.append(inverse)
            brow = {jj: take(b[jj]) for jj in range(j + 1, STRIP)}
            brows.append(brow)
            for jj in range(j + 1, STRIP):
                b[jj] = b[jj] - f * brow[jj]
            rows.append(take(r))
            qrows.append(take(q))
            r = r - f * rows[-1]
            q = q - f * qrows[-1]
        y[s] = q * lax.sqrt(scale)
        for t in range(s + 1, n):
            c = [column(a[t], j) for j in range(STRIP)]
            at, yt = a[t], y[t]
            for j in range(STRIP):
                f = c[j] * pivots[j]
                for jj in range(j + 1, STRIP):
                    c[jj] = c[jj] - f * brows[j][jj]
                at = at - f * rows[j]
                yt = yt - f * qrows[j]
            a[t], y[t] = at, yt
    return jnp.concatenate(y, axis=0)


def factor_inverse(points, jit_row, s_ref, y_ref, between):
    tile = points.shape[0]
    sq = squares_of(points)
    s_ref[...] = on_diagonal(gram_of(points, points, sq, as_row(sq)), 0, jit_row)
    rows = lax.broadcasted_iota(jnp.int32, (tile, tile), 0)
    cols = lax.broadcasted_iota(jnp.int32, (tile, tile), 1)
    y_ref[...] = jnp.where(rows == cols, 1.0, 0.0).astype(jnp.float32)

    def step(block, carry):
        here = pl.ds(pl.multiple_of(block * BLOCK, BLOCK), BLOCK)
        v = invert_block(s_ref[here, here])
        u = dot_n(v, s_ref[here, :])
        x = dot_n(v, y_ref[here, :])
        below = dot_t(s_ref[:, here], v, precision=lax.Precision.HIGHEST)
        ids = lax.broadcasted_iota(jnp.int32, below.shape, 0)
        below = jnp.where(ids >= (block + 1) * BLOCK, below, 0.0)
        s_ref[...] -= dot_n(below, u)
        y_ref[...] -= dot_n(below, x)
        y_ref[here, :] = x
        between(block)
        return carry

    lax.fori_loop(0, tile // BLOCK, step, 0)


def schur_kernel(per_row, rows_ref, cols_ref, first_ref, xh_ref, xl_ref, jit_ref, first_jit_ref,
                 panel_ref, schur_ref, col_row_ref, first_row_ref, ph_ref, pl_ref):
    step = pl.program_id(0)
    row_index = lax.axis_index("row")
    col_index = lax.axis_index("col")
    bm = rows_ref.shape[0]
    tile = cols_ref.shape[0]
    row_start = (row_index * pl.num_programs(0) + step) * bm
    col_start = col_index * tile
    inverse = (xh_ref[...], xl_ref[...])

    @pl.when(step == 0)
    def _():
        col_sq = squares_of(cols_ref[...])
        col_row_ref[...] = as_row(col_sq)
        first_row_ref[...] = as_row(squares_of(first_ref[...]))
        part = gram_of(cols_ref[...], first_ref[...], col_sq, first_row_ref[...])
        part = on_diagonal(part, -col_start, first_jit_ref[0:1, :])
        ph_ref[...], pl_ref[...] = split(dot3_t(split(part), inverse))

    points = rows_ref[...]
    sq = squares_of(points)
    part = gram_of(points, first_ref[...], sq, first_row_ref[...])
    part = on_diagonal(part, -row_start, first_jit_ref[0:1, :])
    panel = dot3_t(split(part), inverse)
    panel_ref[...] = panel
    block = gram_of(points, cols_ref[...], sq, col_row_ref[...])
    block = on_diagonal(block, col_start - row_start, jit_ref[0:1, :])
    schur_ref[...] = block - dot3_t(split(panel), (ph_ref[...], pl_ref[...]))


def schur_call(per_row, row_pts, col_pts, first_pts, xh, xl, jit, first_jit):
    rowb, width = row_pts.shape
    tile = col_pts.shape[0]
    bm = min(1024, rowb)
    whole = lambda shape: pl.BlockSpec(shape, lambda i: (0, 0))
    out = jax.ShapeDtypeStruct((rowb, tile), jnp.float32)
    return pl.pallas_call(
        functools.partial(schur_kernel, per_row),
        grid=(rowb // bm,),
        in_specs=[
            pl.BlockSpec((bm, width), lambda i: (i, 0)),
            whole((tile, width)),
            whole((tile, width)),
            whole((tile, tile)),
            whole((tile, tile)),
            whole((8, tile)),
            whole((8, tile)),
        ],
        out_specs=[pl.BlockSpec((bm, tile), lambda i: (i, 0))] * 2,
        out_shape=(out, out),
        scratch_shapes=[
            pltpu.VMEM((1, tile), jnp.float32),
            pltpu.VMEM((1, tile), jnp.float32),
            pltpu.VMEM((tile, tile), jnp.bfloat16),
            pltpu.VMEM((tile, tile), jnp.bfloat16),
        ],
        compiler_params=pltpu.CompilerParams(vmem_limit_bytes=48 << 20),
        name="schur",
    )(row_pts, col_pts, first_pts, xh, xl, jit, first_jit)


def gather_kernel(rows, cols, own_ref, jit_ref, out_ref, col_ref, first_ref, first_jit_ref,
                  high_ref, low_ref, s_ref, y_ref, send_up, send_down, send_y, send_k, recv,
                  send_x, recv_x, send_f, recv_f, send_fk, send_j, recv_j, local):
    me_row = lax.axis_index("row")
    me = lax.axis_index("col")
    size = own_ref.shape[0]
    tile = col_ref.shape[0]
    spc = tile // size
    per_row = cols // rows
    y_parts = cols // (Z_PARTS * CORES)
    core = lax.rem(me, CORES)
    my_y = lax.rem(me // CORES, y_parts)
    my_z = me // (CORES * y_parts)
    sibling = me + 1 - 2 * core
    chunk = size // CHUNKS

    def index(z, y, k):
        return (z * y_parts + y) * CORES + k

    def y_peer(d):
        return lax.rem(my_y + d, y_parts)

    def row_peer(d):
        return lax.rem(me_row + d, rows)

    shard = me_row * cols + me
    tile_of = shard // spc
    place = lax.rem(shard, spc)
    home = me // per_row

    def part(ref, i, h):
        return ref.at[pl.ds(pl.multiple_of(i * size + h * chunk, chunk), chunk)]

    def whole(ref, i):
        return ref.at[pl.ds(pl.multiple_of(i * size, size), size)]

    def tell(row, col):
        pl.semaphore_signal(barrier, inc=1, device_id=(row, col), device_id_type=MESH)

    barrier = pltpu.get_barrier_semaphore()
    tell(me_row, sibling)

    @pl.when(my_z > 0)
    def _():
        tell(me_row, index(my_z - 1, my_y, core))

    @pl.when(my_z < Z_PARTS - 1)
    def _():
        tell(me_row, index(my_z + 1, my_y, core))

    for d in range(1, y_parts):
        tell(me_row, index(my_z, y_peer(d), core))
    for d in range(1, rows):
        tell(row_peer(d), me)
    for i in range(spc):
        source = me * spc + i
        source_row = source // cols

        @pl.when(source_row != me_row)
        def _():
            tell(source_row, lax.rem(source, cols))

    @pl.when(me != 0)
    def _():
        tell(me_row, 0)

    inner = 1 + 2 + (y_parts - 1) + 2 * (rows - 1)
    ends = (Z_PARTS - 1) * CORES * y_parts

    @pl.when(me == 0)
    def _():
        pl.semaphore_wait(barrier, inner - 1 + cols - 1)

    @pl.when((me != 0) & ((my_z == 0) | (me >= ends)))
    def _():
        pl.semaphore_wait(barrier, inner - 1)

    @pl.when((my_z > 0) & (me < ends))
    def _():
        pl.semaphore_wait(barrier, inner)

    def remote(src, dst, send, recv_sem, row, col):
        return pltpu.make_async_remote_copy(
            src_ref=src, dst_ref=dst, send_sem=send, recv_sem=recv_sem,
            device_id=(row, col), device_id_type=MESH,
        )

    def landed(dst, recv_sem):
        remote(dst, dst, send_j.at[0], recv_sem, me_row, sibling).wait_recv()

    def up(src, z, i, h):
        return remote(src, part(out_ref, i, h), send_up.at[z, h], recv.at[i, h],
                      me_row, index(my_z + 1, my_y, core))

    def down(src, z, i, h):
        return remote(src, part(out_ref, i, h), send_down.at[z, h], recv.at[i, h],
                      me_row, index(my_z - 1, my_y, core))

    def aside(src, z, d, i, h):
        return remote(src, part(out_ref, i, h), send_y.at[z, d, h], recv.at[i, h],
                      me_row, index(my_z, y_peer(d), core))

    def across(src, z, y, h):
        i = index(z, y, core)
        return remote(src, part(out_ref, i, h), send_k.at[z, y, h], recv.at[i, h],
                      me_row, sibling)

    ahead = spc // CORES

    def first_copy(src, d, s, h):
        return remote(src, part(first_ref, s, h), send_f.at[d, s, h], recv_f.at[s, h], d, me)

    def first_across(s, h):
        return remote(part(first_ref, s, h), part(first_ref, s, h), send_fk.at[s, h],
                      recv_f.at[s, h], me_row, sibling)

    def first_rows(src, s, h):
        @pl.when(me_row == 0)
        def _():
            for d in range(1, rows):
                first_copy(src, d, s, h).start()

    def first_aside(h):
        for y in range(ahead):
            s = index(0, y, core)

            @pl.when(my_y != y)
            def _():
                landed(part(out_ref, s, h), recv.at[s, h])
                first_rows(part(out_ref, s, h), s, h)
                across(part(out_ref, s, h), 0, y, h).start()

    def own_up(act, z):
        for h in range(CHUNKS):
            act(up(part(own_ref, 0, h), z, me, h))

    def walk(act, wait):
        def spread(here, z, h):
            i = index(z, my_y, core)
            src = part(out_ref, i, h)
            if wait:
                landed(src, recv.at[i, h])
            if z < here < Z_PARTS - 1:
                act(up(src, z, i, h))
            if z > here > 0:
                act(down(src, z, i, h))
            if wait and z == 0:
                @pl.when(my_y < ahead)
                def _():
                    first_rows(src, i, h)
            for d in range(1, y_parts):
                act(aside(src, z, d, i, h))
            act(across(src, z, my_y, h))

        for here in range(Z_PARTS):
            @pl.when(my_z == here)
            def _():
                if wait and here == 0:
                    for h in range(CHUNKS):
                        first_aside(h)
                for z in ORDER[here]:
                    for h in range(CHUNKS):
                        spread(here, z, h)
                    if z == 0 and here == 1:
                        own_up(act, here)
                    if z == 0 and wait:
                        for h in range(CHUNKS):
                            first_aside(h)

    def own_copies(act, begins):
        for here in range(Z_PARTS - 1):
            if here != 1:
                @pl.when(my_z == here)
                def _():
                    own_up(act, here)
        for h in range(CHUNKS):
            src = part(own_ref, 0, h)
            if begins:
                @pl.when(me < spc)
                def _():
                    first_rows(src, me, h)

            @pl.when(my_z > 0)
            def _():
                act(down(src, my_z, me, h))

            for d in range(1, y_parts):
                act(aside(src, my_z, d, me, h))
            act(across(src, my_z, my_y, h))

    def to_columns(d):
        return remote(own_ref, whole(col_ref, place), send_x.at[d], recv_x.at[place],
                      row_peer(d), tile_of)

    def jit_copy(c):
        return remote(jit_ref, first_jit_ref, send_j.at[c], recv_j, me_row, c)

    def begin(copy):
        copy.start()

    def finish(copy):
        copy.wait_send()

    own_copies(begin, True)
    mine = pltpu.make_async_copy(own_ref, whole(out_ref, me), local.at[0])
    mine.start()

    @pl.when(me == 0)
    def _():
        for c in range(1, cols):
            jit_copy(c).start()
        copy = pltpu.make_async_copy(jit_ref, first_jit_ref, local.at[1])
        copy.start()
        copy.wait()

    walk(begin, True)
    mine.wait()

    for y in range(ahead):
        s = index(0, y, core)
        for h in range(CHUNKS):
            @pl.when(me_row != 0)
            def _():
                landed(part(first_ref, s, h), recv_f.at[s, h])
                first_across(s, h).start()

    for d in range(1, rows):
        to_columns(d).start()

    for y in range(ahead):
        s = index(0, y, 1 - core)
        for h in range(CHUNKS):
            landed(part(out_ref, s, h), recv.at[s, h])

            @pl.when(me_row != 0)
            def _():
                landed(part(first_ref, s, h), recv_f.at[s, h])

    @pl.when(me_row == 0)
    def _():
        copy = pltpu.make_async_copy(out_ref.at[pl.ds(0, tile)], first_ref, local.at[2])
        copy.start()
        copy.wait()

    @pl.when(me != 0)
    def _():
        landed(first_jit_ref, recv_j)

    def pass_on(z):
        for d in range(1, y_parts):
            y = y_peer(d)
            i = index(z, y, core)

            @pl.when(i >= spc)
            def _():
                for h in range(CHUNKS):
                    landed(part(out_ref, i, h), recv.at[i, h])
                    across(part(out_ref, i, h), z, y, h).start()

    blocks = tile // BLOCK

    def between(block):
        @pl.when(block < Z_PARTS)
        def _():
            pass_on(block)

    factor_inverse(first_ref[...], first_jit_ref[0:1, :], s_ref, y_ref, between)
    high_ref[...], low_ref[...] = split(y_ref[...])
    for z in range(blocks, Z_PARTS):
        pass_on(z)

    for z in range(Z_PARTS):
        for y in range(y_parts):
            if index(z, y, 0) >= spc:
                i = index(z, y, 1 - core)
                for h in range(CHUNKS):
                    landed(part(out_ref, i, h), recv.at[i, h])

    @pl.when(home == me_row)
    def _():
        start = pl.multiple_of(lax.rem(me, per_row) * tile, tile)
        copy = pltpu.make_async_copy(out_ref.at[pl.ds(start, tile)], col_ref, local.at[3])
        copy.start()
        copy.wait()

    @pl.when(home != me_row)
    def _():
        for i in range(spc):
            landed(whole(col_ref, i), recv_x.at[i])

    own_copies(finish, False)
    walk(finish, False)
    for z in range(Z_PARTS):
        for d in range(1, y_parts):
            for h in range(CHUNKS):
                y = y_peer(d)
                finish(across(part(out_ref, index(z, y, core), h), z, y, h))
    for d in range(1, rows):
        finish(to_columns(d))
    for y in range(ahead):
        s = index(0, y, core)
        for h in range(CHUNKS):
            @pl.when(me_row == 0)
            def _():
                for d in range(1, rows):
                    finish(first_copy(part(out_ref, s, h), d, s, h))

            @pl.when(me_row != 0)
            def _():
                finish(first_across(s, h))

    @pl.when(me == 0)
    def _():
        for c in range(1, cols):
            finish(jit_copy(c))


def gather_call(rows, cols, landmarks, jit):
    size, width = landmarks.shape
    tile = jit.shape[1]
    spc = tile // size
    y_parts = cols // (Z_PARTS * CORES)
    dma = pltpu.SemaphoreType.DMA
    vmem = pl.BlockSpec(memory_space=pltpu.VMEM)
    hbm = pl.BlockSpec(memory_space=pl.ANY)
    return pl.pallas_call(
        functools.partial(gather_kernel, rows, cols),
        in_specs=[hbm, vmem],
        out_specs=[hbm, hbm, vmem, vmem, vmem, vmem],
        out_shape=(
            jax.ShapeDtypeStruct((cols * size, width), landmarks.dtype),
            jax.ShapeDtypeStruct((tile, width), landmarks.dtype),
            jax.ShapeDtypeStruct((tile, width), landmarks.dtype),
            jax.ShapeDtypeStruct(jit.shape, jit.dtype),
            jax.ShapeDtypeStruct((tile, tile), jnp.bfloat16),
            jax.ShapeDtypeStruct((tile, tile), jnp.bfloat16),
        ),
        scratch_shapes=[
            pltpu.VMEM((tile, tile), jnp.float32),
            pltpu.VMEM((tile, tile), jnp.float32),
            dma((Z_PARTS, CHUNKS)),
            dma((Z_PARTS, CHUNKS)),
            dma((Z_PARTS, y_parts, CHUNKS)),
            dma((Z_PARTS, y_parts, CHUNKS)),
            dma((cols, CHUNKS)),
            dma((rows,)),
            dma((spc,)),
            dma((rows, spc, CHUNKS)),
            dma((spc, CHUNKS)),
            dma((spc, CHUNKS)),
            dma((cols,)),
            dma,
            dma((4,)),
        ],
        compiler_params=pltpu.CompilerParams(
            collective_id=0, has_side_effects=True, vmem_limit_bytes=32 << 20
        ),
        name="gather",
    )(landmarks, jit)


def local(landmarks, jitter):
    rows = lax.axis_size("row")
    cols = lax.axis_size("col")
    tile = jitter.shape[0]
    jit = jnp.broadcast_to(jitter.astype(jnp.float32)[None, :], (8, tile))
    row_pts, col_pts, first_pts, first_jit, xh, xl = gather_call(rows, cols, landmarks, jit)
    return tuple(schur_call(cols // rows, row_pts, col_pts, first_pts, xh, xl, jit, first_jit))


def solution(mesh):
    in_specs = (P(("row", "col"), None), P("col"))
    out_specs = (P("row", None), P("row", "col"))
    return jax.shard_map(local, mesh=mesh, in_specs=in_specs, out_specs=out_specs, check_vma=False)
```
